512 devices in a mesh: pipe: 4 (over x), ctx: 16 (over z, core), tp: 8 (over y).
Axes of the slice: x: 4, y: 8, z: 8, core: 2. Of those that a mesh axis runs over, the one named last changes fastest.
Arguments:
- values: bfloat16 [4, 4096, 8192], P('pipe', 'ctx', 'tp'), may hold values from -6 to 6
- gates: bfloat16 [4, 4096, 8192], P('pipe', 'ctx', 'tp'), may hold values from -6 to 6
- incoming: bfloat16 [4, 4096, 8192], P('pipe', 'ctx', 'tp'), may hold values from -6 to 6
- filters: bfloat16 [4, 512, 128], P('pipe', 'tp'), may hold values from -0.5 to 0.5
- doc_lengths: int32 [16], replicated, may hold values from 1 to 384, 4096 in all
Outputs:
- value_grad: bfloat16 [4, 4096, 8192], P('pipe', 'ctx', 'tp')
- gate_grad: bfloat16 [4, 4096, 8192], P('pipe', 'ctx', 'tp')
- filter_grad: float32 [4, 512, 128], P('pipe', 'tp')
The draws below stay inside these ranges and needn't reach their ends.
All inputs are finite; a program needn't handle non-finite values.
Results may differ from the reference program's by a relative error of at most 0.0049.
Values may be sent and summed in bfloat16 or wider, within the bound.
A program may use at most 64 MiB of HBM per device.

```python
import math
import jax
import jax.numpy as jnp
import numpy as np
from jax import lax

D = 8192
TAPS = 128
BLOCK = 128
GROUPS = 512
SECTIONS = 4
SEQ = 4096
DOCS = 16
MOST = 384


def steps_of(stream_key, extent, split, least, largest):
    loudness = 1.0
    for axis_at, shards_of in split:
        steps = jax.random.uniform(jax.random.fold_in(jax.random.fold_in(stream_key, 6), axis_at), (shards_of,), jnp.float32, least / len(split), largest / len(split))
        loudness = loudness * jnp.repeat(jnp.exp(steps), extent[axis_at] // shards_of).reshape((-1,) + (1,) * (len(extent) - 1 - axis_at))
    return loudness


def profile(count, total, most, skew):
    weights = [(1 << 20) // math.isqrt(rank ** skew) + 1 for rank in range(2, count + 1)]
    surplus, given = total - most - (count - 1), [1] * (count - 1)
    while surplus > 0:
        movable = [i for i in range(count - 1) if given[i] < most]
        whole, left = sum([weights[i] for i in movable]), surplus
        for i in movable:
            extra = min(most - given[i], max(1, left * weights[i] // whole), surplus)
            given[i] = given[i] + extra
            surplus = surplus - extra
    return np.array([most] + given)


def ragged_sizes(rng, amount, total, most, slope):
    if amount == 2:
        one = jax.random.randint(rng, (), max(1, total - most), min(most, total - 1) + 1)
        return jnp.stack([one, total - one])
    lengths = jnp.asarray(profile(amount, total, most, slope), jnp.int32)
    couples = (amount - 1) // 2
    source_of, taker = lengths[1:1 + 2 * couples:2], lengths[2:2 + 2 * couples:2]
    room = jnp.minimum(source_of - 1, most - taker)
    moved = jax.random.randint(jax.random.fold_in(rng, 1), (couples,), 0, 1 << 20) % (room + 1)
    lengths = lengths.at[1:1 + 2 * couples:2].set(source_of - moved).at[2:2 + 2 * couples:2].set(taker + moved)
    return lengths[jax.random.permutation(jax.random.fold_in(rng, 2), amount)]


def noise(stream_key, shape, scale, most, pieces=(), held_as=jnp.bfloat16):
    factor_of = steps_of(stream_key, shape, pieces, -0.22, 0.18) if pieces else 1.0
    entries = jax.random.normal(stream_key, shape, jnp.float32) * scale * factor_of
    return jnp.minimum(jnp.maximum(entries, -most), most).astype(held_as)


def setup_inputs(seed: int = 0) -> dict:
    splits = jax.random.split(jax.random.key(seed), 6)
    return {
        "values": noise(splits[0], (SECTIONS, SEQ, D), 1.0, 6.0, ((0, 4), (1, 16), (2, 8))),
        "gates": noise(splits[1], (SECTIONS, SEQ, D), 1.0, 6.0, ((0, 4), (1, 16), (2, 8))),
        "incoming": noise(splits[2], (SECTIONS, SEQ, D), 1.0, 6.0, ((0, 4), (1, 16), (2, 8))),
        "filters": noise(splits[3], (SECTIONS, GROUPS, TAPS), TAPS ** -0.5, 0.5, ((0, 4), (1, 8))),
        "doc_lengths": ragged_sizes(splits[4], DOCS, SEQ, MOST, 2).astype(jnp.int32),
    }


def band_table(filt, blk, taps):
    win = blk + taps - 1
    rowpos = jnp.arange(blk, dtype=jnp.int32)[:, None]
    colpos = jnp.arange(win, dtype=jnp.int32)[None, :]
    lag = rowpos - colpos + taps - 1
    valid = (lag >= 0) & (lag < taps)
    table = filt[:, jnp.clip(lag, 0, taps - 1)]
    return jnp.where(valid[None], table, jnp.zeros_like(table))


def block_mask(begin, blk, win, starts):
    rim = win - blk
    here = begin + jnp.arange(blk, dtype=jnp.int32)
    source = begin - rim + jnp.arange(win, dtype=jnp.int32)
    before = starts[None, :] <= here[:, None]
    owning = jnp.max(jnp.where(before, starts[None, :], 0), axis=1)
    return source[None, :] >= owning[:, None]


def forward_conv(extended, table, starts, first, rows):
    groups, blk, win = table.shape
    width = extended.shape[1]
    chans = width // groups

    def one(index):
        window = lax.dynamic_slice_in_dim(extended, index * blk, win, 0).reshape(win, groups, chans)
        mask = block_mask(first + index * blk, blk, win, starts)
        weights = jnp.where(mask[None], table, jnp.zeros_like(table))
        part = jnp.einsum("gij,jgc->igc", weights.astype(jnp.float32), window.astype(jnp.float32))
        return part.reshape(blk, width)

    out = lax.map(one, jnp.arange(rows // blk, dtype=jnp.int32))
    return out.reshape(rows, width)


def transpose_conv(grads, table, starts, first, rows):
    groups, blk, win = table.shape
    width = grads.shape[1]
    chans = width // groups
    rim = win - blk

    def step(index, total):
        part = lax.dynamic_slice_in_dim(grads, index * blk, blk, 0).reshape(blk, groups, chans)
        mask = block_mask(first + index * blk, blk, win, starts)
        weights = jnp.where(mask[None], table, jnp.zeros_like(table))
        contrib = jnp.einsum("gij,igc->jgc", weights.astype(jnp.float32), part.astype(jnp.float32)).reshape(win, width)
        older = lax.dynamic_slice_in_dim(total, index * blk, win, 0)
        return lax.dynamic_update_slice_in_dim(total, older + contrib, index * blk, 0)

    start_total = jnp.zeros((rows + rim, width), jnp.float32)
    return lax.fori_loop(0, rows // blk, step, start_total)


def lag_sums(product, blk, win, taps):
    groups = product.shape[0]
    flat = product.reshape(groups, blk * win)
    flat = jnp.concatenate([flat, jnp.zeros((groups, blk), jnp.float32)], axis=1)
    skewed = flat.reshape(groups, blk, win + 1)[:, :, :taps]
    return jnp.flip(jnp.sum(skewed, axis=1), axis=1)


def filter_terms(grads, extended, starts, first, rows, groups, blk, taps):
    win = blk + taps - 1
    width = grads.shape[1]
    chans = width // groups

    def step(index, total):
        part = lax.dynamic_slice_in_dim(grads, index * blk, blk, 0).reshape(blk, groups, chans)
        window = lax.dynamic_slice_in_dim(extended, index * blk, win, 0).reshape(win, groups, chans)
        mask = block_mask(first + index * blk, blk, win, starts)
        product = jnp.einsum("igc,jgc->gij", part.astype(jnp.float32), window.astype(jnp.float32))
        product = jnp.where(mask[None], product, jnp.zeros_like(product))
        return total + lag_sums(product, blk, win, taps)

    return lax.fori_loop(0, rows // blk, step, jnp.zeros((groups, taps), jnp.float32))


def reference(values, gates, incoming, filters, doc_lengths):
    starts = (jnp.cumsum(doc_lengths) - doc_lengths).astype(jnp.int32)
    received = jnp.roll(incoming, -1, axis=0)
    rim = TAPS - 1
    value_list, gate_list, filter_list = [], [], []
    for section in range(SECTIONS):
        current = values[section]
        out_grad = received[section]
        extended = jnp.concatenate([jnp.zeros((rim, D), current.dtype), current], axis=0)
        table = band_table(filters[section], BLOCK, TAPS)
        conv = forward_conv(extended, table, starts, 0, SEQ)
        gate_grad = (out_grad.astype(jnp.float32) * conv).astype(jnp.bfloat16)
        conv_grad = (out_grad.astype(jnp.float32) * gates[section].astype(jnp.float32)).astype(jnp.bfloat16)
        total = transpose_conv(conv_grad, table, starts, 0, SEQ)
        value_list.append(total[rim:].astype(jnp.bfloat16))
        gate_list.append(gate_grad)
        filter_list.append(filter_terms(conv_grad, extended, starts, 0, SEQ, GROUPS, BLOCK, TAPS))
    return jnp.stack(value_list), jnp.stack(gate_list), jnp.stack(filter_list)
```

```python
import functools

import jax
import jax.numpy as jnp
from jax import lax
from jax.experimental import pallas as pl
from jax.experimental.pallas import tpu as pltpu
from jax.sharding import PartitionSpec as P

MESH = pl.DeviceIdType.MESH
TILE = 128
F32 = jnp.float32
BF16 = jnp.bfloat16
LAG = 2


def iota(shape, axis):
    return lax.broadcasted_iota(jnp.int32, shape, axis)


def owner_of(position, starts):
    owner = jnp.zeros_like(position)
    for start in starts[1:]:
        owner = jnp.where(position >= start, start, owner)
    return owner


def dot(left, right, contract):
    return lax.dot_general(left, right, ((contract[0], contract[1]), ((), ())), preferred_element_type=F32)


def kernel(
    n_pipe, n_ctx, chans,
    values, gates, incoming, filters, lengths,
    value_grad, gate_grad, filter_grad,
    v_all, g_all, og, cg_all, conv, gg, vg, filt, lens,
    mask_c, mask_t, mask_q, ahead, back, lhs_c, lhs_t, lhs_p, part, gathered, total,
    load_sem, og_send, og_recv, vh_send, vh_recv, ch_send, ch_recv,
    rs_send, rs_recv, ag_send, ag_recv, out_sem, last_sem,
):
    pipe, me = lax.axis_index("pipe"), lax.axis_index("ctx")
    rows, width = g_all.shape
    blocks = rows // TILE
    tiles = width // TILE
    per = TILE // chans
    groups = filt.shape[0]
    piece = groups // n_ctx
    pipe_prev = lax.rem(pipe + n_pipe - 1, n_pipe)
    pipe_next = lax.rem(pipe + 1, n_pipe)
    prev, nxt = lax.rem(me + n_ctx - 1, n_ctx), lax.rem(me + 1, n_ctx)

    loads = [
        pltpu.make_async_copy(values.at[0], v_all.at[pl.ds(TILE, rows)], load_sem.at[0]),
        pltpu.make_async_copy(gates.at[0], g_all, load_sem.at[1]),
        pltpu.make_async_copy(filters.at[0], filt, load_sem.at[2]),
        pltpu.make_async_copy(lengths, lens, load_sem.at[3]),
    ]
    for load in loads:
        load.start()

    barrier = pltpu.get_barrier_semaphore()
    pl.semaphore_signal(barrier, inc=1, device_id={"pipe": pipe_prev}, device_id_type=MESH)
    pl.semaphore_signal(barrier, inc=1, device_id={"pipe": pipe_next}, device_id_type=MESH)

    def greet(d, carry):
        other = lax.rem(me + d, n_ctx)
        pl.semaphore_signal(barrier, inc=1, device_id={"ctx": other}, device_id_type=MESH)
        return carry

    lax.fori_loop(1, n_ctx, greet, 0)
    pl.semaphore_wait(barrier, n_ctx + 1)

    def columns(ct):
        return pl.ds(pl.multiple_of(ct * TILE, TILE), TILE)

    def og_copy(ct):
        return pltpu.make_async_remote_copy(
            src_ref=incoming.at[0, :, columns(ct)], dst_ref=og.at[:, columns(ct)],
            send_sem=og_send.at[ct], recv_sem=og_recv.at[ct],
            device_id={"pipe": pipe_prev}, device_id_type=MESH,
        )

    def ch_copy(ct):
        return pltpu.make_async_remote_copy(
            src_ref=cg_all.at[pl.ds(0, TILE), columns(ct)],
            dst_ref=cg_all.at[pl.ds(rows, TILE), columns(ct)],
            send_sem=ch_send.at[ct], recv_sem=ch_recv.at[ct],
            device_id={"ctx": prev}, device_id_type=MESH,
        )

    def gg_out(ct):
        return pltpu.make_async_copy(gg.at[:, columns(ct)], gate_grad.at[0, :, columns(ct)], out_sem.at[0, ct])

    def vg_out(ct):
        return pltpu.make_async_copy(vg.at[:, columns(ct)], value_grad.at[0, :, columns(ct)], out_sem.at[1, ct])

    halo = pltpu.make_async_remote_copy(
        src_ref=values.at[0, pl.ds(rows - TILE, TILE)], dst_ref=v_all.at[pl.ds(0, TILE)],
        send_sem=vh_send, recv_sem=vh_recv, device_id={"ctx": nxt}, device_id_type=MESH,
    )
    halo.start()

    def og_start(ct, carry):
        og_copy(ct).start()
        return carry

    lax.fori_loop(0, tiles, og_start, 0)

    loads[3].wait()
    starts, at = [], 0
    for d in range(lens.shape[0]):
        starts.append(at)
        at = at + lens[d]
    first = me * rows
    low = iota((TILE, TILE), 0)
    lane = iota((TILE, TILE), 1)
    for b in range(blocks):
        begin = first + b * TILE
        owner = owner_of(begin + low, starts)
        before = (lane > low) & (begin - TILE + lane >= owner)
        same = (lane <= low) & (begin + lane >= owner)
        mask_q[b, :, :TILE] = jnp.where(before, 1.0, 0.0)
        mask_q[b, :, TILE:] = jnp.where(same, 1.0, 0.0)
        mask_c[b, :, :TILE] = jnp.where(before, 1.0, 0.0).astype(BF16)
        mask_c[b, :, TILE:] = jnp.where(same, 1.0, 0.0).astype(BF16)
        source = begin + low
        for half in range(2):
            target = begin + half * TILE + lane
            side = (lane >= low) if half == 0 else (lane < low)
            keep = side & (source >= owner_of(target, starts)) & (target < n_ctx * rows)
            mask_t[b, :, half * TILE:(half + 1) * TILE] = jnp.where(keep, 1.0, 0.0).astype(BF16)

    loads[2].wait()
    flip = jnp.where(lax.rem(low + lane, TILE) == 0, 1.0, 0.0)
    taps = filt[...]
    ahead[...] = taps.astype(F32).reshape(ahead.shape)
    back[...] = dot(taps, flip.astype(BF16), ((1,), (0,))).reshape(back.shape)

    def circulant(row):
        spread = jnp.broadcast_to(row, (TILE, TILE))
        return pltpu.roll(spread, 0, 1, stride=1, stride_axis=0).astype(BF16)

    lane_group = lane // chans

    def pick(product):
        out = product[0:TILE]
        for g in range(1, per):
            out = jnp.where(lane_group >= g, product[g * TILE:(g + 1) * TILE], out)
        return out

    loads[0].wait()
    halo.wait_recv()

    def conv_step(ct, carry):
        rev = back[ct]
        for g in range(per):
            tile = circulant(rev[g:g + 1])
            for b in range(blocks):
                lhs_c[b, g * TILE:(g + 1) * TILE, :TILE] = tile * mask_c[b, :, :TILE]
                lhs_c[b, g * TILE:(g + 1) * TILE, TILE:] = tile * mask_c[b, :, TILE:]
        for b in range(blocks):
            window = v_all[b * TILE:(b + 2) * TILE, columns(ct)]
            conv[b * TILE:(b + 1) * TILE, columns(ct)] = pick(dot(lhs_c[b], window, ((1,), (0,))))
        fwd = ahead[ct]
        for g in range(per):
            tile = circulant(fwd[g:g + 1])
            for b in range(blocks):
                lhs_t[ct, b, g * TILE:(g + 1) * TILE, :TILE] = tile * mask_t[b, :, :TILE]
                lhs_t[ct, b, g * TILE:(g + 1) * TILE, TILE:] = tile * mask_t[b, :, TILE:]
        return carry

    lax.fori_loop(0, tiles, conv_step, 0)
    loads[1].wait()

    def value_step(ct):
        ch_copy(ct).wait_recv()
        for b in range(blocks):
            window = cg_all[b * TILE:(b + 2) * TILE, columns(ct)]
            vg[b * TILE:(b + 1) * TILE, columns(ct)] = pick(dot(lhs_t[ct, b], window, ((1,), (0,)))).astype(BF16)
        vg_out(ct).start()

    sub = iota((per * 8, TILE), 0) % 8

    def main_step(ct, carry):
        og_copy(ct).wait_recv()
        grad = og[:, columns(ct)].astype(F32)
        cg_all[0:rows, columns(ct)] = (grad * g_all[:, columns(ct)].astype(F32)).astype(BF16)
        ch_copy(ct).start()
        gg[:, columns(ct)] = (grad * conv[:, columns(ct)]).astype(BF16)
        gg_out(ct).start()
        for b in range(blocks):
            own = cg_all[b * TILE:(b + 1) * TILE, columns(ct)]
            for g in range(per):
                keep = (lane_group == g).astype(F32).astype(BF16)
                lhs_p[b, g * TILE:(g + 1) * TILE] = own * keep
        products = []
        for b in range(blocks):
            window = v_all[b * TILE:(b + 2) * TILE, columns(ct)]
            products.append(dot(lhs_p[b], window, ((1,), (1,))))
        skewed = []
        for g in range(per):
            acc = jnp.zeros((8, TILE), F32)
            for a in range(TILE // 8):
                at = slice(a * 8, a * 8 + 8)
                row = slice(g * TILE + a * 8, g * TILE + a * 8 + 8)
                both = jnp.zeros((8, TILE), F32)
                for b in range(blocks):
                    both = both + products[b][row, :TILE] * mask_q[b, at, :TILE]
                    both = both + products[b][row, TILE:] * mask_q[b, at, TILE:]
                acc = acc + pltpu.roll(both, (TILE - 8 * a) % TILE, 1)
            skewed.append(acc)
        table = jnp.concatenate(skewed, axis=0)
        for bit in (1, 2, 4):
            table = jnp.where(sub & bit != 0, pltpu.roll(table, TILE - bit, 1), table)
        sums = jnp.sum(table.reshape(per, 8, TILE), axis=1)
        if piece >= per:
            part[ct // (piece // per), pl.ds(lax.rem(ct, piece // per) * per, per)] = sums
        else:
            for q in range(per // piece):
                part[ct * (per // piece) + q] = sums[q * piece:(q + 1) * piece]

        @pl.when(ct >= LAG)
        def _():
            value_step(ct - LAG)

        return carry

    lax.fori_loop(0, tiles, main_step, 0)

    def rs_copy(to, slot):
        return pltpu.make_async_remote_copy(
            src_ref=part.at[to], dst_ref=gathered.at[slot],
            send_sem=rs_send.at[to], recv_sem=rs_recv.at[slot],
            device_id={"ctx": to}, device_id_type=MESH,
        )

    def ag_copy(to, slot):
        return pltpu.make_async_remote_copy(
            src_ref=total.at[me], dst_ref=total.at[slot],
            send_sem=ag_send.at[to], recv_sem=ag_recv.at[slot],
            device_id={"ctx": to}, device_id_type=MESH,
        )

    def others(act):
        def step(d, carry):
            act(lax.rem(me + d, n_ctx))
            return carry

        lax.fori_loop(1, n_ctx, step, 0)

    others(lambda to: rs_copy(to, me).start())
    gathered[me] = part[me]
    for ct in range(tiles - LAG, tiles - 1):
        value_step(ct)
    others(lambda source: rs_copy(source, source).wait_recv())
    summed = jnp.sum(gathered[...], axis=0)
    total[me] = lax.dot_general(
        summed, flip, (((1,), (0,)), ((), ())), precision=lax.Precision.HIGHEST, preferred_element_type=F32
    )
    others(lambda to: ag_copy(to, me).start())
    value_step(tiles - 1)
    others(lambda source: ag_copy(source, source).wait_recv())
    last = pltpu.make_async_copy(total, filter_grad, last_sem)
    last.start()

    halo.wait_send()

    def finish(ct, carry):
        og_copy(ct).wait_send()
        ch_copy(ct).wait_send()
        gg_out(ct).wait()
        vg_out(ct).wait()
        return carry

    lax.fori_loop(0, tiles, finish, 0)
    others(lambda to: rs_copy(to, me).wait_send())
    others(lambda to: ag_copy(to, me).wait_send())
    last.wait()


def solution(mesh):
    n_pipe, n_ctx = mesh.shape["pipe"], mesh.shape["ctx"]

    def body(values, gates, incoming, filters, lengths):
        _, rows, width = values.shape
        _, groups, taps = filters.shape
        tiles, blocks = width // TILE, rows // TILE
        chans = width // groups
        per = TILE // chans
        piece = groups // n_ctx
        dma = pltpu.SemaphoreType.DMA
        any_spec = pl.BlockSpec(memory_space=pl.ANY)
        value_grad, gate_grad, filter_grad = pl.pallas_call(
            functools.partial(kernel, n_pipe, n_ctx, chans),
            out_shape=(
                jax.ShapeDtypeStruct(values.shape, BF16),
                jax.ShapeDtypeStruct(values.shape, BF16),
                jax.ShapeDtypeStruct((n_ctx, piece, taps), F32),
            ),
            in_specs=[any_spec] * 5,
            out_specs=(any_spec,) * 3,
            scratch_shapes=[
                pltpu.VMEM((rows + TILE, width), BF16),
                pltpu.VMEM((rows, width), BF16),
                pltpu.VMEM((rows, width), BF16),
                pltpu.VMEM((rows + TILE, width), BF16),
                pltpu.VMEM((rows, width), F32),
                pltpu.VMEM((rows, width), BF16),
                pltpu.VMEM((rows, width), BF16),
                pltpu.VMEM((groups, taps), BF16),
                pltpu.SMEM(lengths.shape, jnp.int32),
                pltpu.VMEM((blocks, TILE, 2 * TILE), BF16),
                pltpu.VMEM((blocks, TILE, 2 * TILE), BF16),
                pltpu.VMEM((blocks, TILE, 2 * TILE), F32),
                pltpu.VMEM((tiles, per, taps), F32),
                pltpu.VMEM((tiles, per, taps), F32),
                pltpu.VMEM((blocks, per * TILE, 2 * TILE), BF16),
                pltpu.VMEM((tiles, blocks, per * TILE, 2 * TILE), BF16),
                pltpu.VMEM((blocks, per * TILE, TILE), BF16),
                pltpu.VMEM((n_ctx, piece, taps), F32),
                pltpu.VMEM((n_ctx, piece, taps), F32),
                pltpu.VMEM((n_ctx, piece, taps), F32),
                dma((4,)),
                dma((tiles,)), dma((tiles,)),
                dma, dma,
                dma((tiles,)), dma((tiles,)),
                dma((n_ctx,)), dma((n_ctx,)),
                dma((n_ctx,)), dma((n_ctx,)),
                dma((2, tiles)), dma,
            ],
            compiler_params=pltpu.CompilerParams(
                collective_id=0, has_side_effects=True, vmem_limit_bytes=48 * 1024 * 1024
            ),
            cost_estimate=pl.CostEstimate(
                flops=2 * 3 * groups * blocks * TILE * 2 * TILE * TILE,
                bytes_accessed=5 * rows * width * 2, transcendentals=0,
            ),
        )(values, gates, incoming, filters, lengths)
        return value_grad, gate_grad, filter_grad.reshape(filters.shape)

    shards = P("pipe", "ctx", "tp")
    taps = P("pipe", "tp", None)
    return jax.shard_map(
        body, mesh=mesh, in_specs=(shards, shards, shards, taps, P()), out_specs=(shards, shards, taps), check_vma=False
    )
```

```python
import functools

import jax
import jax.numpy as jnp
from jax import lax
from jax.experimental import pallas as pl
from jax.experimental.pallas import tpu as pltpu
from jax.sharding import PartitionSpec as P

MESH = pl.DeviceIdType.MESH
TILE = 128
F32 = jnp.float32
BF16 = jnp.bfloat16


def iota(shape, axis):
    return lax.broadcasted_iota(jnp.int32, shape, axis)


def owner_of(position, starts):
    owner = jnp.zeros_like(position)
    for start in starts[1:]:
        owner = jnp.where(position >= start, start, owner)
    return owner


def dot(left, right, contract):
    return lax.dot_general(left, right, ((contract[0], contract[1]), ((), ())), preferred_element_type=F32)


def kernel(
    n_pipe, n_ctx, chans,
    values, gates, incoming, filters, lengths,
    value_grad, gate_grad, filter_grad,
    v_all, g_all, og, cg_all, conv, gg, vg, filt, lens,
    mask_c, mask_t, mask_q, ahead, back, lhs_c, lhs_t, lhs_p, slots, mine, theirs, total,
    load_sem, og_send, og_recv, vh_send, vh_recv, ch_send, ch_recv,
    z_send, z_recv, pair_send, pair_recv, out_sem, last_sem, near_sem,
):
    pipe, me = lax.axis_index("pipe"), lax.axis_index("ctx")
    rows, width = g_all.shape
    blocks = rows // TILE
    tiles = width // TILE
    per = TILE // chans
    groups = filt.shape[0]
    n_z = n_ctx // 2
    z = me // 2
    partner = me + 1 - 2 * (me % 2)
    pipe_prev = lax.rem(pipe + n_pipe - 1, n_pipe)
    pipe_next = lax.rem(pipe + 1, n_pipe)
    prev, nxt = lax.rem(me + n_ctx - 1, n_ctx), lax.rem(me + 1, n_ctx)

    loads = [
        pltpu.make_async_copy(values.at[0], v_all.at[pl.ds(TILE, rows)], load_sem.at[0]),
        pltpu.make_async_copy(gates.at[0], g_all, load_sem.at[1]),
        pltpu.make_async_copy(filters.at[0], filt, load_sem.at[2]),
        pltpu.make_async_copy(lengths, lens, load_sem.at[3]),
    ]
    for load in loads:
        load.start()

    barrier = pltpu.get_barrier_semaphore()
    pl.semaphore_signal(barrier, inc=1, device_id={"pipe": pipe_prev}, device_id_type=MESH)
    pl.semaphore_signal(barrier, inc=1, device_id={"pipe": pipe_next}, device_id_type=MESH)

    pl.semaphore_signal(barrier, inc=1, device_id={"ctx": prev}, device_id_type=MESH)
    pl.semaphore_signal(barrier, inc=1, device_id={"ctx": nxt}, device_id_type=MESH)
    pl.semaphore_wait(barrier, 4)

    rounds = (n_ctx // 2).bit_length() - 1

    def tell(r):
        for other in (me + n_ctx - (1 << r), me + (1 << r)):
            pl.semaphore_signal(near_sem.at[r], inc=1, device_id={"ctx": lax.rem(other, n_ctx)}, device_id_type=MESH)

    def hear(r):
        pl.semaphore_wait(near_sem.at[r], 2)
        if r + 1 < rounds:
            tell(r + 1)

    def columns(ct):
        return pl.ds(pl.multiple_of(ct * TILE, TILE), TILE)

    def og_copy(ct):
        return pltpu.make_async_remote_copy(
            src_ref=incoming.at[0, :, columns(ct)], dst_ref=og.at[:, columns(ct)],
            send_sem=og_send.at[ct], recv_sem=og_recv.at[ct],
            device_id={"pipe": pipe_prev}, device_id_type=MESH,
        )

    def ch_copy(ct):
        return pltpu.make_async_remote_copy(
            src_ref=cg_all.at[pl.ds(0, TILE), columns(ct)],
            dst_ref=cg_all.at[pl.ds(rows, TILE), columns(ct)],
            send_sem=ch_send.at[ct], recv_sem=ch_recv.at[ct],
            device_id={"ctx": prev}, device_id_type=MESH,
        )

    def gg_out(ct):
        return pltpu.make_async_copy(gg.at[:, columns(ct)], gate_grad.at[0, :, columns(ct)], out_sem.at[0, ct])

    def vg_out(ct):
        return pltpu.make_async_copy(vg.at[:, columns(ct)], value_grad.at[0, :, columns(ct)], out_sem.at[1, ct])

    halo = pltpu.make_async_remote_copy(
        src_ref=values.at[0, pl.ds(rows - TILE, TILE)], dst_ref=v_all.at[pl.ds(0, TILE)],
        send_sem=vh_send, recv_sem=vh_recv, device_id={"ctx": nxt}, device_id_type=MESH,
    )
    halo.start()

    og_copy(0).start()
    og_copy(1).start()
    tell(0)

    loads[3].wait()
    starts, at = [], 0
    for d in range(lens.shape[0]):
        starts.append(at)
        at = at + lens[d]
    first = me * rows
    low = iota((TILE, TILE), 0)
    lane = iota((TILE, TILE), 1)
    for b in range(blocks):
        begin = first + b * TILE
        owner = owner_of(begin + low, starts)
        before = (lane > low) & (begin - TILE + lane >= owner)
        same = (lane <= low) & (begin + lane >= owner)
        mask_q[b, :, :TILE] = jnp.where(before, 1.0, 0.0)
        mask_q[b, :, TILE:] = jnp.where(same, 1.0, 0.0)
        mask_c[b, :, :TILE] = jnp.where(before, 1.0, 0.0).astype(BF16)
        mask_c[b, :, TILE:] = jnp.where(same, 1.0, 0.0).astype(BF16)
        source = begin + low
        for half in range(2):
            target = begin + half * TILE + lane
            side = (lane >= low) if half == 0 else (lane < low)
            keep = side & (source >= owner_of(target, starts)) & (target < n_ctx * rows)
            mask_t[b, :, half * TILE:(half + 1) * TILE] = jnp.where(keep, 1.0, 0.0).astype(BF16)

    loads[2].wait()
    flip = jnp.where(lax.rem(low + lane, TILE) == 0, 1.0, 0.0)
    taps = filt[...]
    ahead[...] = taps.astype(F32).reshape(ahead.shape)
    back[...] = dot(taps, flip.astype(BF16), ((1,), (0,))).reshape(back.shape)

    def circulant(row):
        spread = jnp.broadcast_to(row, (TILE, TILE))
        return pltpu.roll(spread, 0, 1, stride=1, stride_axis=0).astype(BF16)

    lane_group = lane // chans

    def pick(product):
        out = product[0:TILE]
        for g in range(1, per):
            out = jnp.where(lane_group >= g, product[g * TILE:(g + 1) * TILE], out)
        return out

    loads[0].wait()

    def convolve(ct, b):
        window = v_all[b * TILE:(b + 2) * TILE, columns(ct)]
        conv[b * TILE:(b + 1) * TILE, columns(ct)] = pick(dot(lhs_c[ct, b], window, ((1,), (0,))))

    def conv_step(ct, carry):
        @pl.when((ct == 2) | (ct == 5))
        def _():
            og_copy(ct // 5 + 2).start()

        for r in range(rounds - 1):
            pl.when(ct == 3 * r + 2)(functools.partial(hear, r))

        rev, fwd = back[ct], ahead[ct]
        for g in range(per):
            at = slice(g * TILE, (g + 1) * TILE)
            tile = circulant(rev[g:g + 1])
            for b in range(blocks):
                lhs_c[ct, b, at, :TILE] = tile * mask_c[b, :, :TILE]
                lhs_c[ct, b, at, TILE:] = tile * mask_c[b, :, TILE:]
            tile = circulant(fwd[g:g + 1])
            for b in range(blocks):
                lhs_t[ct, b, at, :TILE] = tile * mask_t[b, :, :TILE]
                lhs_t[ct, b, at, TILE:] = tile * mask_t[b, :, TILE:]
        for b in range(1, blocks):
            convolve(ct, b)
        return carry

    def first_step(ct, carry):
        convolve(ct, 0)
        return carry

    lax.fori_loop(0, tiles, conv_step, 0)
    halo.wait_recv()
    lax.fori_loop(0, tiles, first_step, 0)
    hear(rounds - 1)
    loads[1].wait()

    def value_step(ct):
        ch_copy(ct).wait_recv()
        for b in range(blocks):
            window = cg_all[b * TILE:(b + 2) * TILE, columns(ct)]
            vg[b * TILE:(b + 1) * TILE, columns(ct)] = pick(dot(lhs_t[ct, b], window, ((1,), (0,)))).astype(BF16)
        vg_out(ct).start()

    def z_copy(ct, k):
        return pltpu.make_async_remote_copy(
            src_ref=slots.at[ct, z], dst_ref=slots.at[ct, z],
            send_sem=z_send.at[ct, k], recv_sem=z_recv.at[ct, k],
            device_id={"ctx": lax.rem(me + 2 * k, n_ctx)}, device_id_type=MESH,
        )

    def z_wait(ct, k):
        source = lax.rem(z + n_z - k, n_z)
        pltpu.make_async_remote_copy(
            src_ref=slots.at[ct, source], dst_ref=slots.at[ct, source],
            send_sem=z_send.at[ct, k], recv_sem=z_recv.at[ct, k],
            device_id={"ctx": lax.rem(me + 2 * k, n_ctx)}, device_id_type=MESH,
        ).wait_recv()

    def pair_copy(ct):
        return pltpu.make_async_remote_copy(
            src_ref=mine.at[ct], dst_ref=theirs.at[ct],
            send_sem=pair_send.at[ct], recv_sem=pair_recv.at[ct],
            device_id={"ctx": partner}, device_id_type=MESH,
        )

    def column_sum(ct):
        for k in range(1, n_z):
            z_wait(ct, k)
        mine[ct] = jnp.sum(slots[ct], axis=0)
        pair_copy(ct).start()

    sub = iota((per * 8, TILE), 0) % 8

    def main_step(ct, carry):
        @pl.when(ct < tiles - 4)
        def _():
            og_copy(ct + 4).start()

        og_copy(ct).wait_recv()
        grad = og[:, columns(ct)].astype(F32)
        cg_all[0:rows, columns(ct)] = (grad * g_all[:, columns(ct)].astype(F32)).astype(BF16)
        ch_copy(ct).start()
        gg[:, columns(ct)] = (grad * conv[:, columns(ct)]).astype(BF16)
        gg_out(ct).start()
        for b in range(blocks):
            own = cg_all[b * TILE:(b + 1) * TILE, columns(ct)]
            for g in range(per):
                keep = (lane_group == g).astype(F32).astype(BF16)
                lhs_p[b, g * TILE:(g + 1) * TILE] = own * keep
        products = []
        for b in range(blocks):
            window = v_all[b * TILE:(b + 2) * TILE, columns(ct)]
            products.append(dot(lhs_p[b], window, ((1,), (1,))))
        skewed = []
        for g in range(per):
            acc = jnp.zeros((8, TILE), F32)
            for a in range(TILE // 8):
                at = slice(a * 8, a * 8 + 8)
                row = slice(g * TILE + a * 8, g * TILE + a * 8 + 8)
                both = jnp.zeros((8, TILE), F32)
                for b in range(blocks):
                    both = both + products[b][row, :TILE] * mask_q[b, at, :TILE]
                    both = both + products[b][row, TILE:] * mask_q[b, at, TILE:]
                acc = acc + pltpu.roll(both, (TILE - 8 * a) % TILE, 1)
            skewed.append(acc)
        table = jnp.concatenate(skewed, axis=0)
        for bit in (1, 2, 4):
            table = jnp.where(sub & bit != 0, pltpu.roll(table, TILE - bit, 1), table)
        sums = jnp.sum(table.reshape(per, 8, TILE), axis=1)
        slots[ct, z] = sums
        for k in range(1, n_z):
            z_copy(ct, k).start()

        return carry

    lax.fori_loop(0, tiles, main_step, 0)

    def tail_step(ct, carry):
        value_step(ct)
        column_sum(ct)
        return carry

    lax.fori_loop(0, tiles - 1, tail_step, 0)
    value_step(tiles - 1)
    column_sum(tiles - 1)
    for ct in range(tiles):
        pair_copy(ct).wait_recv()
    both = (mine[...] + theirs[...]).reshape(groups, TILE)
    total[...] = lax.dot_general(
        both, flip, (((1,), (0,)), ((), ())), precision=lax.Precision.HIGHEST, preferred_element_type=F32
    )
    last = pltpu.make_async_copy(total, filter_grad.at[0], last_sem)
    last.start()

    halo.wait_send()

    def finish(ct, carry):
        og_copy(ct).wait_send()
        ch_copy(ct).wait_send()
        gg_out(ct).wait()
        vg_out(ct).wait()
        pair_copy(ct).wait_send()
        for k in range(1, n_z):
            z_copy(ct, k).wait_send()
        return carry

    lax.fori_loop(0, tiles, finish, 0)
    last.wait()


def solution(mesh):
    n_pipe, n_ctx = mesh.shape["pipe"], mesh.shape["ctx"]

    def body(values, gates, incoming, filters, lengths):
        _, rows, width = values.shape
        _, groups, taps = filters.shape
        tiles, blocks = width // TILE, rows // TILE
        chans = width // groups
        per = TILE // chans
        n_z = n_ctx // 2
        dma = pltpu.SemaphoreType.DMA
        any_spec = pl.BlockSpec(memory_space=pl.ANY)
        value_grad, gate_grad, filter_grad = pl.pallas_call(
            functools.partial(kernel, n_pipe, n_ctx, chans),
            out_shape=(
                jax.ShapeDtypeStruct(values.shape, BF16),
                jax.ShapeDtypeStruct(values.shape, BF16),
                jax.ShapeDtypeStruct(filters.shape, F32),
            ),
            in_specs=[pl.BlockSpec(memory_space=pltpu.HBM)] * 5,
            out_specs=(any_spec,) * 3,
            scratch_shapes=[
                pltpu.VMEM((rows + TILE, width), BF16),
                pltpu.VMEM((rows, width), BF16),
                pltpu.VMEM((rows, width), BF16),
                pltpu.VMEM((rows + TILE, width), BF16),
                pltpu.VMEM((rows, width), F32),
                pltpu.VMEM((rows, width), BF16),
                pltpu.VMEM((rows, width), BF16),
                pltpu.VMEM((groups, taps), BF16),
                pltpu.SMEM(lengths.shape, jnp.int32),
                pltpu.VMEM((blocks, TILE, 2 * TILE), BF16),
                pltpu.VMEM((blocks, TILE, 2 * TILE), BF16),
                pltpu.VMEM((blocks, TILE, 2 * TILE), F32),
                pltpu.VMEM((tiles, per, taps), F32),
                pltpu.VMEM((tiles, per, taps), F32),
                pltpu.VMEM((tiles, blocks, per * TILE, 2 * TILE), BF16),
                pltpu.VMEM((tiles, blocks, per * TILE, 2 * TILE), BF16),
                pltpu.VMEM((blocks, per * TILE, TILE), BF16),
                pltpu.VMEM((tiles, n_z, per, taps), F32),
                pltpu.VMEM((tiles, per, taps), F32),
                pltpu.VMEM((tiles, per, taps), F32),
                pltpu.VMEM((groups, taps), F32),
                dma((4,)),
                dma((tiles,)), dma((tiles,)),
                dma, dma,
                dma((tiles,)), dma((tiles,)),
                dma((tiles, n_z)), dma((tiles, n_z)),
                dma((tiles,)), dma((tiles,)),
                dma((2, tiles)), dma,
                pltpu.SemaphoreType.REGULAR((4,)),
            ],
            compiler_params=pltpu.CompilerParams(
                collective_id=0, has_side_effects=True, vmem_limit_bytes=62 * 1024 * 1024
            ),
            cost_estimate=pl.CostEstimate(
                flops=2 * 3 * groups * blocks * TILE * 2 * TILE * TILE,
                bytes_accessed=5 * rows * width * 2, transcendentals=0,
            ),
        )(values, gates, incoming, filters, lengths)
        return value_grad, gate_grad, filter_grad

    shards = P("pipe", "ctx", "tp")
    taps = P("pipe", "tp", None)
    return jax.shard_map(
        body, mesh=mesh, in_specs=(shards, shards, shards, taps, P()), out_specs=(shards, shards, taps), check_vma=False
    )
```

```python
import functools

import jax
import jax.numpy as jnp
from jax import lax
from jax.experimental import pallas as pl
from jax.experimental.pallas import tpu as pltpu
from jax.sharding import PartitionSpec as P

MESH = pl.DeviceIdType.MESH
TILE = 128
F32 = jnp.float32
BF16 = jnp.bfloat16


def iota(shape, axis):
    return lax.broadcasted_iota(jnp.int32, shape, axis)


def owner_of(position, starts):
    owner = jnp.zeros_like(position)
    for start in starts[1:]:
        owner = jnp.where(position >= start, start, owner)
    return owner


def dot(left, right, contract):
    return lax.dot_general(left, right, ((contract[0], contract[1]), ((), ())), preferred_element_type=F32)


def kernel(
    n_pipe, n_ctx, chans,
    values, gates, incoming, filters, lengths,
    value_grad, gate_grad, filter_grad,
    v_all, g_all, og, cg_all, conv, filt, lens,
    mask_c, mask_t, mask_q, ahead, back, lhs_a, lhs_b, lhs_c, lhs_t, lhs_p, slots, mine, theirs,
    load_sem, og_send, og_recv, vh_send, vh_recv, ch_send, ch_recv,
    z_send, z_recv, pair_send, pair_recv, near_sem,
):
    pipe, me = lax.axis_index("pipe"), lax.axis_index("ctx")
    rows, width = g_all.shape
    blocks = rows // TILE
    tiles = width // TILE
    per = TILE // chans
    groups = filt.shape[0]
    n_z = n_ctx // 2
    z = me // 2
    partner = me + 1 - 2 * (me % 2)
    pipe_prev = lax.rem(pipe + n_pipe - 1, n_pipe)
    pipe_next = lax.rem(pipe + 1, n_pipe)
    prev, nxt = lax.rem(me + n_ctx - 1, n_ctx), lax.rem(me + 1, n_ctx)

    loads = [
        pltpu.make_async_copy(values.at[0], v_all.at[pl.ds(TILE, rows)], load_sem.at[0]),
        pltpu.make_async_copy(gates.at[0], g_all, load_sem.at[1]),
        pltpu.make_async_copy(filters.at[0], filt, load_sem.at[2]),
        pltpu.make_async_copy(lengths, lens, load_sem.at[3]),
    ]
    for load in loads:
        load.start()

    barrier = pltpu.get_barrier_semaphore()
    pl.semaphore_signal(barrier, inc=1, device_id={"pipe": pipe_prev}, device_id_type=MESH)
    pl.semaphore_signal(barrier, inc=1, device_id={"pipe": pipe_next}, device_id_type=MESH)

    pl.semaphore_signal(barrier, inc=1, device_id={"ctx": prev}, device_id_type=MESH)
    pl.semaphore_signal(barrier, inc=1, device_id={"ctx": nxt}, device_id_type=MESH)
    pl.semaphore_wait(barrier, 4)

    rounds = (n_ctx // 2).bit_length() - 1

    def tell(r):
        for other in (me + n_ctx - (1 << r), me + (1 << r)):
            pl.semaphore_signal(near_sem.at[r], inc=1, device_id={"ctx": lax.rem(other, n_ctx)}, device_id_type=MESH)

    def hear(r):
        pl.semaphore_wait(near_sem.at[r], 2)
        if r + 1 < rounds:
            tell(r + 1)

    def columns(ct):
        return pl.ds(pl.multiple_of(ct * TILE, TILE), TILE)

    def wide(cp):
        return pl.ds(pl.multiple_of(cp * 2 * TILE, 2 * TILE), 2 * TILE)

    def og_copy(ct):
        return pltpu.make_async_remote_copy(
            src_ref=incoming.at[0, :, columns(ct)], dst_ref=og.at[:, columns(ct)],
            send_sem=og_send, recv_sem=og_recv.at[ct],
            device_id={"pipe": pipe_prev}, device_id_type=MESH,
        )

    def ch_copy(cp):
        return pltpu.make_async_remote_copy(
            src_ref=cg_all.at[pl.ds(0, TILE), wide(cp)],
            dst_ref=cg_all.at[pl.ds(rows, TILE), wide(cp)],
            send_sem=ch_send, recv_sem=ch_recv.at[cp],
            device_id={"ctx": prev}, device_id_type=MESH,
        )

    def halo(cp):
        return pltpu.make_async_remote_copy(
            src_ref=values.at[0, pl.ds(rows - TILE, TILE), wide(cp)], dst_ref=v_all.at[pl.ds(0, TILE), wide(cp)],
            send_sem=vh_send, recv_sem=vh_recv.at[cp], device_id={"ctx": nxt}, device_id_type=MESH,
        )

    halo(0).start()
    og_copy(0).start()
    tell(0)
    for cp in range(1, tiles // 2):
        halo(cp).start()
    og_copy(1).start()

    loads[3].wait()
    starts, at = [], 0
    for d in range(lens.shape[0]):
        starts.append(at)
        at = at + lens[d]
    first = me * rows
    low = iota((TILE, TILE), 0)
    lane = iota((TILE, TILE), 1)
    for b in range(blocks):
        begin = first + b * TILE
        owner = owner_of(begin + low, starts)
        before = (lane > low) & (begin - TILE + lane >= owner)
        same = (lane <= low) & (begin + lane >= owner)
        mask_q[b, :, :TILE] = jnp.where(before, 1.0, 0.0)
        mask_q[b, :, TILE:] = jnp.where(same, 1.0, 0.0)
        mask_c[b, :, :TILE] = jnp.where(before, 1.0, 0.0).astype(BF16)
        mask_c[b, :, TILE:] = jnp.where(same, 1.0, 0.0).astype(BF16)
        source = begin + low
        for half in range(2):
            target = begin + half * TILE + lane
            side = (lane >= low) if half == 0 else (lane < low)
            keep = side & (source >= owner_of(target, starts)) & (target < n_ctx * rows)
            mask_t[b, :, half * TILE:(half + 1) * TILE] = jnp.where(keep, 1.0, 0.0).astype(BF16)

    loads[2].wait()
    flip = jnp.where(lax.rem(low + lane, TILE) == 0, 1.0, 0.0)
    taps = filt[...]
    ahead[...] = taps.astype(F32).reshape(ahead.shape)
    back[...] = dot(taps, flip.astype(BF16), ((1,), (0,))).reshape(back.shape)

    def circulant(row):
        spread = jnp.broadcast_to(row, (TILE, TILE))
        return pltpu.roll(spread, 0, 1, stride=1, stride_axis=0).astype(BF16)

    lane_group = lane // chans

    def pick(product):
        out = product[0:TILE]
        for g in range(1, per):
            out = jnp.where(lane_group >= g, product[g * TILE:(g + 1) * TILE], out)
        return out

    loads[0].wait()

    def tables(ct, own):
        rev, fwd = back[ct], ahead[ct]
        for g in range(per):
            at = slice(g * TILE, (g + 1) * TILE)
            tile = circulant(rev[g:g + 1])
            own[at, :TILE] = tile * mask_c[1, :, :TILE]
            own[at, TILE:] = tile * mask_c[1, :, TILE:]
            lhs_c[ct, at, :TILE] = tile * mask_c[0, :, :TILE]
            lhs_c[ct, at, TILE:] = tile * mask_c[0, :, TILE:]
            tile = circulant(fwd[g:g + 1])
            for b in range(blocks):
                lhs_t[ct, b, at, :TILE] = tile * mask_t[b, :, :TILE]
                lhs_t[ct, b, at, TILE:] = tile * mask_t[b, :, TILE:]

    def convolve(ct, b, lhs):
        window = v_all[b * TILE:(b + 2) * TILE, columns(ct)]
        conv[b * TILE:(b + 1) * TILE, columns(ct)] = pick(dot(lhs[...], window, ((1,), (0,))))

    tables(0, lhs_a)

    def conv_step(i, carry):
        @pl.when(i == 1)
        def _():
            og_copy(2).start()
            hear(0)

        tables(2 * i + 1, lhs_b)
        convolve(2 * i, 1, lhs_a)
        tables(2 * i + 2, lhs_a)
        convolve(2 * i + 1, 1, lhs_b)
        return carry

    def first_step(cp, carry):
        halo(cp).wait_recv()
        for j in range(2):
            convolve(2 * cp + j, 0, lhs_c.at[2 * cp + j])
        return carry

    lax.fori_loop(0, tiles // 2 - 1, conv_step, 0)
    og_copy(3).start()
    tables(tiles - 1, lhs_b)
    convolve(tiles - 2, 1, lhs_a)
    convolve(tiles - 1, 1, lhs_b)
    og_copy(4).start()
    hear(1)
    lax.fori_loop(0, tiles // 2, first_step, 0)
    og_copy(5).start()
    loads[1].wait()

    def value_step(cp):
        ch_copy(cp).wait_recv()
        for j in range(2):
            ct = 2 * cp + j
            for b in range(blocks):
                window = cg_all[b * TILE:(b + 2) * TILE, columns(ct)]
                product = dot(lhs_t[ct, b], window, ((1,), (0,)))
                value_grad[0, b * TILE:(b + 1) * TILE, columns(ct)] = pick(product).astype(BF16)

    def z_copy(cp, k):
        return pltpu.make_async_remote_copy(
            src_ref=slots.at[cp, z], dst_ref=slots.at[cp, z],
            send_sem=z_send, recv_sem=z_recv.at[cp],
            device_id={"ctx": lax.rem(me + 2 * k, n_ctx)}, device_id_type=MESH,
        )

    def z_all(cp):
        part = slots.at[cp, pl.ds(0, n_z - 1)]
        return pltpu.make_async_remote_copy(
            src_ref=part, dst_ref=part, send_sem=z_send, recv_sem=z_recv.at[cp],
            device_id={"ctx": nxt}, device_id_type=MESH,
        )

    def pair_copy(cp):
        return pltpu.make_async_remote_copy(
            src_ref=mine.at[cp], dst_ref=theirs.at[cp],
            send_sem=pair_send, recv_sem=pair_recv.at[cp],
            device_id={"ctx": partner}, device_id_type=MESH,
        )

    def column_sum(cp):
        z_all(cp).wait_recv()
        mine[cp] = jnp.sum(slots[cp], axis=0)
        pair_copy(cp).start()

    sub = iota((per * 8, TILE), 0) % 8
    keeps = [(lane_group == g).astype(F32).astype(BF16) for g in range(per)]

    def main_step(cp, carry):
        @pl.when(cp < tiles - 6)
        def _():
            og_copy(cp + 6).start()

        @pl.when(cp == 0)
        def _():
            hear(2)

        og_copy(2 * cp).wait_recv()
        og_copy(2 * cp + 1).wait_recv()
        grad = og[:, wide(cp)].astype(F32)
        turned = (grad * g_all[:, wide(cp)].astype(F32)).astype(BF16)
        cg_all[0:rows, wide(cp)] = turned
        ch_copy(cp).start()
        gate_grad[0, :, wide(cp)] = (grad * conv[:, wide(cp)]).astype(BF16)
        for j in range(2):
            for b in range(blocks):
                own = turned[b * TILE:(b + 1) * TILE, j * TILE:(j + 1) * TILE]
                for g in range(per):
                    lhs_p[j, b, g * TILE:(g + 1) * TILE] = own * keeps[g]
        sums = []
        for j in range(2):
            products = []
            for b in range(blocks):
                window = v_all[b * TILE:(b + 2) * TILE, columns(2 * cp + j)]
                products.append(dot(lhs_p[j, b], window, ((1,), (1,))))
            skewed = []
            for g in range(per):
                acc = jnp.zeros((8, TILE), F32)
                for a in range(TILE // 8):
                    at = slice(a * 8, a * 8 + 8)
                    row = slice(g * TILE + a * 8, g * TILE + a * 8 + 8)
                    both = jnp.zeros((8, TILE), F32)
                    for b in range(blocks):
                        both = both + products[b][row, :TILE] * mask_q[b, at, :TILE]
                        both = both + products[b][row, TILE:] * mask_q[b, at, TILE:]
                    acc = acc + pltpu.roll(both, (TILE - 8 * a) % TILE, 1)
                skewed.append(acc)
            table = jnp.concatenate(skewed, axis=0)
            for bit in (1, 2, 4):
                table = jnp.where(sub & bit != 0, pltpu.roll(table, TILE - bit, 1), table)
            sums.append(jnp.sum(table.reshape(per, 8, TILE), axis=1))
        slots[cp, z] = jnp.concatenate(sums, axis=0)
        for k in range(1, n_z):
            z_copy(cp, k).start()
        return carry

    lax.fori_loop(0, tiles // 2, main_step, 0)

    def tail_step(cp, carry):
        value_step(cp)
        column_sum(cp)
        return carry

    lax.fori_loop(0, tiles // 2 - 1, tail_step, 0)
    value_step(tiles // 2 - 1)
    column_sum(tiles // 2 - 1)
    for cp in range(tiles // 2):
        pair_copy(cp).wait_recv()
    both = (mine[...] + theirs[...]).reshape(groups, TILE)
    filter_grad[0] = lax.dot_general(
        both, flip, (((1,), (0,)), ((), ())), precision=lax.Precision.HIGHEST, preferred_element_type=F32
    )

    def sent(ref, sem):
        pltpu.make_async_remote_copy(
            src_ref=ref, dst_ref=ref, send_sem=sem, recv_sem=vh_recv.at[0],
            device_id={"ctx": nxt}, device_id_type=MESH,
        ).wait_send()

    sent(v_all.at[pl.ds(0, TILE)], vh_send)
    sent(og, og_send)
    sent(cg_all.at[pl.ds(0, TILE)], ch_send)
    sent(slots.at[:, pl.ds(0, n_z - 1)], z_send)
    sent(mine, pair_send)


def hand_over(a, b, c, a_out, b_out, c_out, sems):
    parts = 4
    copies = [pltpu.make_async_copy(c, c_out, sems.at[2 * parts])]
    rows = a.shape[1] // parts
    for i in range(parts):
        at = pl.ds(i * rows, rows)
        copies.append(pltpu.make_async_copy(a.at[0, at], a_out.at[0, at], sems.at[i]))
        copies.append(pltpu.make_async_copy(b.at[0, at], b_out.at[0, at], sems.at[parts + i]))
    for copy in copies:
        copy.start()
    for copy in copies:
        copy.wait()


def solution(mesh):
    n_pipe, n_ctx = mesh.shape["pipe"], mesh.shape["ctx"]

    def body(values, gates, incoming, filters, lengths):
        _, rows, width = values.shape
        _, groups, taps = filters.shape
        tiles, blocks = width // TILE, rows // TILE
        chans = width // groups
        per = TILE // chans
        n_z = n_ctx // 2
        dma = pltpu.SemaphoreType.DMA
        any_spec = pl.BlockSpec(memory_space=pl.ANY)
        value_grad, gate_grad, filter_grad = pl.pallas_call(
            functools.partial(kernel, n_pipe, n_ctx, chans),
            out_shape=(
                pltpu.VMEM(values.shape, BF16),
                pltpu.VMEM(values.shape, BF16),
                pltpu.VMEM(filters.shape, F32),
            ),
            in_specs=[pl.BlockSpec(memory_space=pltpu.HBM)] * 5,
            out_specs=(pl.BlockSpec(memory_space=pltpu.VMEM),) * 3,
            scratch_shapes=[
                pltpu.VMEM((rows + TILE, width), BF16),
                pltpu.VMEM((rows, width), BF16),
                pltpu.VMEM((rows, width), BF16),
                pltpu.VMEM((rows + TILE, width), BF16),
                pltpu.VMEM((rows, width), F32),
                pltpu.VMEM((groups, taps), BF16),
                pltpu.SMEM(lengths.shape, jnp.int32),
                pltpu.VMEM((blocks, TILE, 2 * TILE), BF16),
                pltpu.VMEM((blocks, TILE, 2 * TILE), BF16),
                pltpu.VMEM((blocks, TILE, 2 * TILE), F32),
                pltpu.VMEM((tiles, per, taps), F32),
                pltpu.VMEM((tiles, per, taps), F32),
                pltpu.VMEM((per * TILE, 2 * TILE), BF16),
                pltpu.VMEM((per * TILE, 2 * TILE), BF16),
                pltpu.VMEM((tiles, per * TILE, 2 * TILE), BF16),
                pltpu.VMEM((tiles, blocks, per * TILE, 2 * TILE), BF16),
                pltpu.VMEM((2, blocks, per * TILE, TILE), BF16),
                pltpu.VMEM((tiles // 2, n_z, 2 * per, taps), F32),
                pltpu.VMEM((tiles // 2, 2 * per, taps), F32),
                pltpu.VMEM((tiles // 2, 2 * per, taps), F32),
                dma((4,)),
                dma, dma((tiles,)),
                dma, dma((tiles // 2,)),
                dma, dma((tiles // 2,)),
                dma, dma((tiles // 2,)),
                dma, dma((tiles // 2,)),
                pltpu.SemaphoreType.REGULAR((3,)),
            ],
            compiler_params=pltpu.CompilerParams(
                collective_id=0, has_side_effects=True, vmem_limit_bytes=62 * 1024 * 1024
            ),
            cost_estimate=pl.CostEstimate(
                flops=2 * 3 * groups * blocks * TILE * 2 * TILE * TILE,
                bytes_accessed=5 * rows * width * 2, transcendentals=0,
            ),
        )(values, gates, incoming, filters, lengths)
        results = (value_grad, gate_grad, filter_grad)
        return pl.pallas_call(
            hand_over,
            out_shape=tuple(jax.ShapeDtypeStruct(r.shape, r.dtype) for r in results),
            in_specs=[any_spec] * 3,
            out_specs=(any_spec,) * 3,
            scratch_shapes=[dma((9,))],
            compiler_params=pltpu.CompilerParams(vmem_limit_bytes=4 * 1024 * 1024),
        )(*results)

    shards = P("pipe", "ctx", "tp")
    taps = P("pipe", "tp", None)
    return jax.shard_map(
        body, mesh=mesh, in_specs=(shards, shards, shards, taps, P()), out_specs=(shards, shards, taps), check_vma=False
    )
```

```python
import functools

import jax
import jax.numpy as jnp
from jax import lax
from jax.experimental import pallas as pl
from jax.experimental.pallas import tpu as pltpu
from jax.sharding import PartitionSpec as P

MESH = pl.DeviceIdType.MESH
TILE = 128
F32 = jnp.float32
BF16 = jnp.bfloat16


def iota(shape, axis):
    return lax.broadcasted_iota(jnp.int32, shape, axis)


def owner_of(position, starts):
    owner = jnp.zeros_like(position)
    for start in starts[1:]:
        owner = jnp.where(position >= start, start, owner)
    return owner


def dot(left, right, contract):
    return lax.dot_general(left, right, ((contract[0], contract[1]), ((), ())), preferred_element_type=F32)


def kernel(
    n_pipe, n_ctx, chans,
    values, gates, incoming, filters, lengths,
    value_grad, gate_grad, filter_grad,
    v_all, g_all, og, cg_all, conv, filt, lens,
    mask_c, mask_t, mask_q, ahead, back, lhs_a, lhs_b, lhs_c, lhs_t, lhs_p, slots, mine, theirs,
    load_sem, og_send, og_recv, vh_send, vh_recv, ch_send, ch_recv,
    z_send, z_recv, pair_send, pair_recv, near_sem,
):
    pipe, me = lax.axis_index("pipe"), lax.axis_index("ctx")
    rows, width = g_all.shape
    blocks = rows // TILE
    tiles = width // TILE
    per = TILE // chans
    groups = filt.shape[0]
    n_z = n_ctx // 2
    z = me // 2
    partner = me + 1 - 2 * (me % 2)
    pipe_prev = lax.rem(pipe + n_pipe - 1, n_pipe)
    pipe_next = lax.rem(pipe + 1, n_pipe)
    prev, nxt = lax.rem(me + n_ctx - 1, n_ctx), lax.rem(me + 1, n_ctx)

    loads = [
        pltpu.make_async_copy(values.at[0], v_all.at[pl.ds(TILE, rows)], load_sem.at[0]),
        pltpu.make_async_copy(gates.at[0], g_all, load_sem.at[1]),
        pltpu.make_async_copy(filters.at[0], filt, load_sem.at[2]),
        pltpu.make_async_copy(lengths, lens, load_sem.at[3]),
    ]
    for load in loads:
        load.start()

    barrier = pltpu.get_barrier_semaphore()
    pl.semaphore_signal(barrier, inc=1, device_id={"pipe": pipe_prev}, device_id_type=MESH)
    pl.semaphore_signal(barrier, inc=1, device_id={"pipe": pipe_next}, device_id_type=MESH)

    pl.semaphore_signal(barrier, inc=1, device_id={"ctx": prev}, device_id_type=MESH)
    pl.semaphore_signal(barrier, inc=1, device_id={"ctx": nxt}, device_id_type=MESH)
    pl.semaphore_wait(barrier, 4)

    rounds = (n_ctx // 2).bit_length() - 1

    def tell(r):
        for other in (me + n_ctx - (1 << r), me + (1 << r)):
            pl.semaphore_signal(near_sem.at[r], inc=1, device_id={"ctx": lax.rem(other, n_ctx)}, device_id_type=MESH)

    def hear(r):
        pl.semaphore_wait(near_sem.at[r], 2)
        if r + 1 < rounds:
            tell(r + 1)

    def columns(ct):
        return pl.ds(pl.multiple_of(ct * TILE, TILE), TILE)

    def wide(cp):
        return pl.ds(pl.multiple_of(cp * 2 * TILE, 2 * TILE), 2 * TILE)

    def og_copy(ct):
        return pltpu.make_async_remote_copy(
            src_ref=incoming.at[0, :, columns(ct)], dst_ref=og.at[:, columns(ct)],
            send_sem=og_send, recv_sem=og_recv.at[ct],
            device_id={"pipe": pipe_prev}, device_id_type=MESH,
        )

    def ch_copy(cp):
        return pltpu.make_async_remote_copy(
            src_ref=cg_all.at[pl.ds(0, TILE), wide(cp)],
            dst_ref=cg_all.at[pl.ds(rows, TILE), wide(cp)],
            send_sem=ch_send, recv_sem=ch_recv.at[cp],
            device_id={"ctx": prev}, device_id_type=MESH,
        )

    def halo(cp):
        return pltpu.make_async_remote_copy(
            src_ref=values.at[0, pl.ds(rows - TILE, TILE), wide(cp)], dst_ref=v_all.at[pl.ds(0, TILE), wide(cp)],
            send_sem=vh_send, recv_sem=vh_recv.at[cp], device_id={"ctx": nxt}, device_id_type=MESH,
        )

    og_copy(0).start()
    halo(0).start()
    tell(0)
    for cp in range(1, tiles // 2):
        halo(cp).start()
    og_copy(1).start()

    loads[3].wait()
    starts, at = [], 0
    for d in range(lens.shape[0]):
        starts.append(at)
        at = at + lens[d]
    first = me * rows
    low = iota((TILE, TILE), 0)
    lane = iota((TILE, TILE), 1)
    for b in range(blocks):
        begin = first + b * TILE
        owner = owner_of(begin + low, starts)
        before = (lane > low) & (begin - TILE + lane >= owner)
        same = (lane <= low) & (begin + lane >= owner)
        mask_q[b, :, :TILE] = jnp.where(before, 1.0, 0.0)
        mask_q[b, :, TILE:] = jnp.where(same, 1.0, 0.0)
        mask_c[b, :, :TILE] = jnp.where(before, 1.0, 0.0).astype(BF16)
        mask_c[b, :, TILE:] = jnp.where(same, 1.0, 0.0).astype(BF16)
        source = begin + low
        for half in range(2):
            target = begin + half * TILE + lane
            side = (lane >= low) if half == 0 else (lane < low)
            keep = side & (source >= owner_of(target, starts)) & (target < n_ctx * rows)
            mask_t[b, :, half * TILE:(half + 1) * TILE] = jnp.where(keep, 1.0, 0.0).astype(BF16)

    loads[2].wait()
    flip = jnp.where(lax.rem(low + lane, TILE) == 0, 1.0, 0.0)
    taps = filt[...]
    ahead[...] = taps.astype(F32).reshape(ahead.shape)
    back[...] = dot(taps, flip.astype(BF16), ((1,), (0,))).reshape(back.shape)

    def circulant(row):
        spread = jnp.broadcast_to(row, (TILE, TILE))
        return pltpu.roll(spread, 0, 1, stride=1, stride_axis=0).astype(BF16)

    lane_group = lane // chans

    def pick(product):
        out = product[0:TILE]
        for g in range(1, per):
            out = jnp.where(lane_group >= g, product[g * TILE:(g + 1) * TILE], out)
        return out

    loads[0].wait()

    def tables(ct, own):
        rev, fwd = back[ct], ahead[ct]
        for g in range(per):
            at = slice(g * TILE, (g + 1) * TILE)
            tile = circulant(rev[g:g + 1])
            own[at, :TILE] = tile * mask_c[1, :, :TILE]
            own[at, TILE:] = tile * mask_c[1, :, TILE:]
            lhs_c[ct, at, :TILE] = tile * mask_c[0, :, :TILE]
            lhs_c[ct, at, TILE:] = tile * mask_c[0, :, TILE:]
            tile = circulant(fwd[g:g + 1])
            for b in range(blocks):
                lhs_t[ct, b, at, :TILE] = tile * mask_t[b, :, :TILE]
                lhs_t[ct, b, at, TILE:] = tile * mask_t[b, :, TILE:]

    def convolve(ct, b, lhs):
        window = v_all[b * TILE:(b + 2) * TILE, columns(ct)]
        conv[b * TILE:(b + 1) * TILE, columns(ct)] = pick(dot(lhs[...], window, ((1,), (0,))))

    tables(0, lhs_a)

    def conv_step(i, carry):
        @pl.when(i == 1)
        def _():
            og_copy(2).start()
            hear(0)

        tables(2 * i + 1, lhs_b)
        convolve(2 * i, 1, lhs_a)
        tables(2 * i + 2, lhs_a)
        convolve(2 * i + 1, 1, lhs_b)
        return carry

    def first_step(cp, carry):
        @pl.when(cp == 1)
        def _():
            og_copy(4).start()

        halo(cp).wait_recv()
        for j in range(2):
            convolve(2 * cp + j, 0, lhs_c.at[2 * cp + j])
        return carry

    lax.fori_loop(0, tiles // 2 - 1, conv_step, 0)
    og_copy(3).start()
    tables(tiles - 1, lhs_b)
    convolve(tiles - 2, 1, lhs_a)
    convolve(tiles - 1, 1, lhs_b)
    hear(1)
    lax.fori_loop(0, tiles // 2, first_step, 0)
    og_copy(5).start()
    loads[1].wait()

    def value_step(cp):
        ch_copy(cp).wait_recv()
        for j in range(2):
            ct = 2 * cp + j
            for b in range(blocks):
                window = cg_all[b * TILE:(b + 2) * TILE, columns(ct)]
                product = dot(lhs_t[ct, b], window, ((1,), (0,)))
                value_grad[0, b * TILE:(b + 1) * TILE, columns(ct)] = pick(product).astype(BF16)

    def z_copy(cp, k):
        return pltpu.make_async_remote_copy(
            src_ref=slots.at[cp, z], dst_ref=slots.at[cp, z],
            send_sem=z_send, recv_sem=z_recv.at[cp],
            device_id={"ctx": lax.rem(me + 2 * k, n_ctx)}, device_id_type=MESH,
        )

    def z_all(cp):
        part = slots.at[cp, pl.ds(0, n_z - 1)]
        return pltpu.make_async_remote_copy(
            src_ref=part, dst_ref=part, send_sem=z_send, recv_sem=z_recv.at[cp],
            device_id={"ctx": nxt}, device_id_type=MESH,
        )

    def pair_copy(cp):
        return pltpu.make_async_remote_copy(
            src_ref=mine.at[cp], dst_ref=theirs.at[cp],
            send_sem=pair_send, recv_sem=pair_recv.at[cp],
            device_id={"ctx": partner}, device_id_type=MESH,
        )

    def column_sum(cp):
        z_all(cp).wait_recv()
        mine[cp] = jnp.sum(slots[cp], axis=0)
        pair_copy(cp).start()

    sub = iota((per * 8, TILE), 0) % 8
    keeps = [(lane_group == g).astype(F32).astype(BF16) for g in range(per)]

    def turn(at, cols):
        grad = og[at, cols].astype(F32)
        turned = (grad * g_all[at, cols].astype(F32)).astype(BF16)
        cg_all[at, cols] = turned
        return grad, turned

    def outer(ct, b, own, lhs):
        for g in range(per):
            lhs[g * TILE:(g + 1) * TILE] = own * keeps[g]
        window = v_all[b * TILE:(b + 2) * TILE, columns(ct)]
        return dot(lhs[...], window, ((1,), (1,)))

    def fold(products):
        folded = []
        for g in range(per):
            acc = jnp.zeros((8, TILE), F32)
            for a in range(TILE // 8):
                at = slice(a * 8, a * 8 + 8)
                row = slice(g * TILE + a * 8, g * TILE + a * 8 + 8)
                both = jnp.zeros((8, TILE), F32)
                for b, product in products:
                    both = both + product[row, :TILE] * mask_q[b, at, :TILE]
                    both = both + product[row, TILE:] * mask_q[b, at, TILE:]
                acc = acc + pltpu.roll(both, (TILE - 8 * a) % TILE, 1)
            folded.append(acc)
        return jnp.concatenate(folded, axis=0)

    def unskew(table):
        for bit in (1, 2, 4):
            table = jnp.where(sub & bit != 0, pltpu.roll(table, TILE - bit, 1), table)
        return jnp.sum(table.reshape(per, 8, TILE), axis=1)

    def share(cp, sums):
        slots[cp, z] = jnp.concatenate(sums, axis=0)
        for k in sorted(range(1, n_z), key=lambda k: -min(k, n_z - k)):
            z_copy(cp, k).start()

    def main_step(cp, carry):
        @pl.when(cp == 0)
        def _():
            og_copy(6).start()
            hear(2)

        @pl.when(cp == 1)
        def _():
            og_copy(7).start()

        og_copy(2 * cp).wait_recv()
        og_copy(2 * cp + 1).wait_recv()

        grad, turned = turn(slice(0, rows), wide(cp))
        ch_copy(cp).start()
        gate_grad[0, :, wide(cp)] = (grad * conv[:, wide(cp)]).astype(BF16)
        sums = []
        for j in range(2):
            products = []
            for b in range(blocks):
                own = turned[b * TILE:(b + 1) * TILE, j * TILE:(j + 1) * TILE]
                products.append((b, outer(2 * cp + j, b, own, lhs_p.at[j, b])))
            sums.append(unskew(fold(products)))
        share(cp, sums)
        return carry

    lax.fori_loop(0, tiles // 2, main_step, 0)

    def tail_step(cp, carry):
        value_step(cp)
        column_sum(cp)
        return carry

    lax.fori_loop(0, tiles // 2 - 1, tail_step, 0)
    value_step(tiles // 2 - 1)
    column_sum(tiles // 2 - 1)
    for cp in range(tiles // 2):
        pair_copy(cp).wait_recv()
    filter_grad[0] = (mine[...] + theirs[...]).reshape(groups, TILE)

    def sent(ref, sem):
        pltpu.make_async_remote_copy(
            src_ref=ref, dst_ref=ref, send_sem=sem, recv_sem=vh_recv.at[0],
            device_id={"ctx": nxt}, device_id_type=MESH,
        ).wait_send()

    sent(v_all.at[pl.ds(0, TILE)], vh_send)
    sent(og, og_send)
    sent(cg_all.at[pl.ds(0, TILE)], ch_send)
    sent(slots.at[:, pl.ds(0, n_z - 1)], z_send)
    sent(mine, pair_send)


def hand_over(a, b, c, a_out, b_out, c_out, flipped, sems):
    parts = 4
    copies = []
    rows = a.shape[1] // parts
    for i in range(parts):
        at = pl.ds(i * rows, rows)
        copies.append(pltpu.make_async_copy(a.at[0, at], a_out.at[0, at], sems.at[i]))
        copies.append(pltpu.make_async_copy(b.at[0, at], b_out.at[0, at], sems.at[parts + i]))
    for copy in copies:
        copy.start()
    flip = jnp.where(lax.rem(iota((TILE, TILE), 0) + iota((TILE, TILE), 1), TILE) == 0, 1.0, 0.0)
    flipped[0] = lax.dot_general(
        c[0], flip, (((1,), (0,)), ((), ())), precision=lax.Precision.HIGHEST, preferred_element_type=F32
    )
    copies.append(pltpu.make_async_copy(flipped, c_out, sems.at[2 * parts]))
    copies[-1].start()
    for copy in copies:
        copy.wait()


def solution(mesh):
    n_pipe, n_ctx = mesh.shape["pipe"], mesh.shape["ctx"]

    def body(values, gates, incoming, filters, lengths):
        _, rows, width = values.shape
        _, groups, taps = filters.shape
        tiles, blocks = width // TILE, rows // TILE
        chans = width // groups
        per = TILE // chans
        n_z = n_ctx // 2
        dma = pltpu.SemaphoreType.DMA
        any_spec = pl.BlockSpec(memory_space=pl.ANY)
        value_grad, gate_grad, filter_grad = pl.pallas_call(
            functools.partial(kernel, n_pipe, n_ctx, chans),
            out_shape=(
                pltpu.VMEM(values.shape, BF16),
                pltpu.VMEM(values.shape, BF16),
                pltpu.VMEM(filters.shape, F32),
            ),
            in_specs=[pl.BlockSpec(memory_space=pltpu.HBM)] * 5,
            out_specs=(pl.BlockSpec(memory_space=pltpu.VMEM),) * 3,
            scratch_shapes=[
                pltpu.VMEM((rows + TILE, width), BF16),
                pltpu.VMEM((rows, width), BF16),
                pltpu.VMEM((rows, width), BF16),
                pltpu.VMEM((rows + TILE, width), BF16),
                pltpu.VMEM((rows, width), F32),
                pltpu.VMEM((groups, taps), BF16),
                pltpu.SMEM(lengths.shape, jnp.int32),
                pltpu.VMEM((blocks, TILE, 2 * TILE), BF16),
                pltpu.VMEM((blocks, TILE, 2 * TILE), BF16),
                pltpu.VMEM((blocks, TILE, 2 * TILE), F32),
                pltpu.VMEM((tiles, per, taps), F32),
                pltpu.VMEM((tiles, per, taps), F32),
                pltpu.VMEM((per * TILE, 2 * TILE), BF16),
                pltpu.VMEM((per * TILE, 2 * TILE), BF16),
                pltpu.VMEM((tiles, per * TILE, 2 * TILE), BF16),
                pltpu.VMEM((tiles, blocks, per * TILE, 2 * TILE), BF16),
                pltpu.VMEM((2, blocks, per * TILE, TILE), BF16),
                pltpu.VMEM((tiles // 2, n_z, 2 * per, taps), F32),
                pltpu.VMEM((tiles // 2, 2 * per, taps), F32),
                pltpu.VMEM((tiles // 2, 2 * per, taps), F32),
                dma((4,)),
                dma, dma((tiles,)),
                dma, dma((tiles // 2,)),
                dma, dma((tiles // 2,)),
                dma, dma((tiles // 2,)),
                dma, dma((tiles // 2,)),
                pltpu.SemaphoreType.REGULAR((3,)),
            ],
            compiler_params=pltpu.CompilerParams(
                collective_id=0, has_side_effects=True, vmem_limit_bytes=62 * 1024 * 1024
            ),
            cost_estimate=pl.CostEstimate(
                flops=2 * 3 * groups * blocks * TILE * 2 * TILE * TILE,
                bytes_accessed=5 * rows * width * 2, transcendentals=0,
            ),
        )(values, gates, incoming, filters, lengths)
        results = (value_grad, gate_grad, filter_grad)
        return pl.pallas_call(
            hand_over,
            out_shape=tuple(jax.ShapeDtypeStruct(r.shape, r.dtype) for r in results),
            in_specs=[any_spec, any_spec, pl.BlockSpec(memory_space=pltpu.VMEM)],
            out_specs=(any_spec,) * 3,
            scratch_shapes=[pltpu.VMEM(filters.shape, F32), dma((9,))],
            compiler_params=pltpu.CompilerParams(vmem_limit_bytes=4 * 1024 * 1024),
        )(*results)

    shards = P("pipe", "ctx", "tp")
    taps = P("pipe", "tp", None)
    return jax.shard_map(
        body, mesh=mesh, in_specs=(shards, shards, shards, taps, P()), out_specs=(shards, shards, taps), check_vma=False
    )
```

```python
import functools

import jax
import jax.numpy as jnp
from jax import lax
from jax.experimental import pallas as pl
from jax.experimental.pallas import tpu as pltpu
from jax.sharding import PartitionSpec as P

MESH = pl.DeviceIdType.MESH
TILE = 128
F32 = jnp.float32
BF16 = jnp.bfloat16


def iota(shape, axis):
    return lax.broadcasted_iota(jnp.int32, shape, axis)


def owner_of(position, starts):
    owner = jnp.zeros_like(position)
    for start in starts[1:]:
        owner = jnp.where(position >= start, start, owner)
    return owner


def dot(left, right, contract):
    return lax.dot_general(left, right, ((contract[0], contract[1]), ((), ())), preferred_element_type=F32)


def kernel(
    n_pipe, n_ctx, chans,
    values, gates, incoming, filters, lengths,
    value_grad, gate_grad, filter_grad,
    v_all, g_all, og, cg_all, conv, filt, lens,
    mask_c, mask_t, mask_q, ahead, back, lhs_a, lhs_b, lhs_c, lhs_t, lhs_p, slots, mine, theirs,
    load_sem, og_send, og_recv, vh_send, vh_recv, ch_send, ch_recv,
    z_send, z_recv, pair_send, pair_recv, near_sem,
):
    pipe, me = lax.axis_index("pipe"), lax.axis_index("ctx")
    rows, width = g_all.shape
    blocks = rows // TILE
    tiles = width // TILE
    per = TILE // chans
    groups = filt.shape[0]
    n_z = n_ctx // 2
    z = me // 2
    partner = me + 1 - 2 * (me % 2)
    pipe_prev = lax.rem(pipe + n_pipe - 1, n_pipe)
    pipe_next = lax.rem(pipe + 1, n_pipe)
    prev, nxt = lax.rem(me + n_ctx - 1, n_ctx), lax.rem(me + 1, n_ctx)

    loads = [
        pltpu.make_async_copy(values.at[0], v_all.at[pl.ds(TILE, rows)], load_sem.at[0]),
        pltpu.make_async_copy(gates.at[0], g_all, load_sem.at[1]),
        pltpu.make_async_copy(filters.at[0], filt, load_sem.at[2]),
        pltpu.make_async_copy(lengths, lens, load_sem.at[3]),
    ]
    for load in loads:
        load.start()

    barrier = pltpu.get_barrier_semaphore()
    pl.semaphore_signal(barrier, inc=1, device_id={"pipe": pipe_next}, device_id_type=MESH)

    pl.semaphore_signal(barrier, inc=1, device_id={"ctx": prev}, device_id_type=MESH)
    pl.semaphore_signal(barrier, inc=1, device_id={"ctx": nxt}, device_id_type=MESH)
    pl.semaphore_wait(barrier, 3)

    rounds = (n_ctx // 2).bit_length() - 1

    def tell(r):
        for other in (me + n_ctx - (1 << r), me + (1 << r)):
            pl.semaphore_signal(near_sem.at[r], inc=1, device_id={"ctx": lax.rem(other, n_ctx)}, device_id_type=MESH)

    def hear(r):
        pl.semaphore_wait(near_sem.at[r], 2)
        if r + 1 < rounds:
            tell(r + 1)

    def columns(ct):
        return pl.ds(pl.multiple_of(ct * TILE, TILE), TILE)

    def wide(cp):
        return pl.ds(pl.multiple_of(cp * 2 * TILE, 2 * TILE), 2 * TILE)

    def og_copy(ct):
        return pltpu.make_async_remote_copy(
            src_ref=incoming.at[0, :, columns(ct)], dst_ref=og.at[:, columns(ct)],
            send_sem=og_send, recv_sem=og_recv.at[ct],
            device_id={"pipe": pipe_prev}, device_id_type=MESH,
        )

    def ch_copy(cp):
        return pltpu.make_async_remote_copy(
            src_ref=cg_all.at[pl.ds(0, TILE), wide(cp)],
            dst_ref=cg_all.at[pl.ds(rows, TILE), wide(cp)],
            send_sem=ch_send, recv_sem=ch_recv.at[cp],
            device_id={"ctx": prev}, device_id_type=MESH,
        )

    def halo(cp):
        return pltpu.make_async_remote_copy(
            src_ref=values.at[0, pl.ds(rows - TILE, TILE), wide(cp)], dst_ref=v_all.at[pl.ds(0, TILE), wide(cp)],
            send_sem=vh_send, recv_sem=vh_recv.at[cp], device_id={"ctx": nxt}, device_id_type=MESH,
        )

    og_copy(0).start()
    halo(0).start()
    tell(0)
    for cp in range(1, tiles // 2):
        halo(cp).start()
    og_copy(1).start()

    loads[3].wait()
    starts, at = [], 0
    for d in range(lens.shape[0]):
        starts.append(at)
        at = at + lens[d]
    first = me * rows
    low = iota((TILE, TILE), 0)
    lane = iota((TILE, TILE), 1)
    for b in range(blocks):
        begin = first + b * TILE
        owner = owner_of(begin + low, starts)
        before = (lane > low) & (begin - TILE + lane >= owner)
        same = (lane <= low) & (begin + lane >= owner)
        mask_q[b, :, :TILE] = jnp.where(before, 1.0, 0.0)
        mask_q[b, :, TILE:] = jnp.where(same, 1.0, 0.0)
        mask_c[b, :, :TILE] = jnp.where(before, 1.0, 0.0).astype(BF16)
        mask_c[b, :, TILE:] = jnp.where(same, 1.0, 0.0).astype(BF16)
        source = begin + low
        for half in range(2):
            target = begin + half * TILE + lane
            side = (lane >= low) if half == 0 else (lane < low)
            keep = side & (source >= owner_of(target, starts)) & (target < n_ctx * rows)
            mask_t[b, :, half * TILE:(half + 1) * TILE] = jnp.where(keep, 1.0, 0.0).astype(BF16)

    loads[2].wait()
    flip = jnp.where(lax.rem(low + lane, TILE) == 0, 1.0, 0.0)
    taps = filt[...]
    ahead[...] = taps.astype(F32).reshape(ahead.shape)
    back[...] = dot(taps, flip.astype(BF16), ((1,), (0,))).reshape(back.shape)

    def circulant(row):
        spread = jnp.broadcast_to(row, (TILE, TILE))
        return pltpu.roll(spread, 0, 1, stride=1, stride_axis=0).astype(BF16)

    lane_group = lane // chans

    def pick(product):
        out = product[0:TILE]
        for g in range(1, per):
            out = jnp.where(lane_group >= g, product[g * TILE:(g + 1) * TILE], out)
        return out

    loads[0].wait()

    def tables(ct, own):
        rev, fwd = back[ct], ahead[ct]
        for g in range(per):
            at = slice(g * TILE, (g + 1) * TILE)
            tile = circulant(rev[g:g + 1])
            own[at, :TILE] = tile * mask_c[1, :, :TILE]
            own[at, TILE:] = tile * mask_c[1, :, TILE:]
            lhs_c[ct, at, :TILE] = tile * mask_c[0, :, :TILE]
            lhs_c[ct, at, TILE:] = tile * mask_c[0, :, TILE:]
            tile = circulant(fwd[g:g + 1])
            for b in range(blocks):
                lhs_t[ct, b, at, :TILE] = tile * mask_t[b, :, :TILE]
                lhs_t[ct, b, at, TILE:] = tile * mask_t[b, :, TILE:]

    def convolve(ct, b, lhs):
        window = v_all[b * TILE:(b + 2) * TILE, columns(ct)]
        conv[b * TILE:(b + 1) * TILE, columns(ct)] = pick(dot(lhs[...], window, ((1,), (0,))))

    tables(0, lhs_a)

    def conv_step(i, carry):
        @pl.when(i == 1)
        def _():
            og_copy(2).start()
            hear(0)

        tables(2 * i + 1, lhs_b)
        convolve(2 * i, 1, lhs_a)
        tables(2 * i + 2, lhs_a)
        convolve(2 * i + 1, 1, lhs_b)
        return carry

    def first_step(cp, carry):
        @pl.when(cp == 1)
        def _():
            og_copy(4).start()

        halo(cp).wait_recv()
        for j in range(2):
            convolve(2 * cp + j, 0, lhs_c.at[2 * cp + j])
        return carry

    lax.fori_loop(0, tiles // 2 - 1, conv_step, 0)
    og_copy(3).start()
    tables(tiles - 1, lhs_b)
    convolve(tiles - 2, 1, lhs_a)
    convolve(tiles - 1, 1, lhs_b)
    hear(1)
    lax.fori_loop(0, tiles // 2, first_step, 0)
    og_copy(5).start()
    loads[1].wait()

    def value_step(cp):
        ch_copy(cp).wait_recv()
        for j in range(2):
            ct = 2 * cp + j
            for b in range(blocks):
                window = cg_all[b * TILE:(b + 2) * TILE, columns(ct)]
                product = dot(lhs_t[ct, b], window, ((1,), (0,)))
                value_grad[0, b * TILE:(b + 1) * TILE, columns(ct)] = pick(product).astype(BF16)

    def z_copy(cp, k):
        return pltpu.make_async_remote_copy(
            src_ref=slots.at[cp, z], dst_ref=slots.at[cp, z],
            send_sem=z_send, recv_sem=z_recv.at[cp],
            device_id={"ctx": lax.rem(me + 2 * k, n_ctx)}, device_id_type=MESH,
        )

    def z_all(cp):
        part = slots.at[cp, pl.ds(0, n_z - 1)]
        return pltpu.make_async_remote_copy(
            src_ref=part, dst_ref=part, send_sem=z_send, recv_sem=z_recv.at[cp],
            device_id={"ctx": nxt}, device_id_type=MESH,
        )

    def pair_copy(cp):
        return pltpu.make_async_remote_copy(
            src_ref=mine.at[cp], dst_ref=theirs.at[cp],
            send_sem=pair_send, recv_sem=pair_recv.at[cp],
            device_id={"ctx": partner}, device_id_type=MESH,
        )

    def column_sum(cp):
        z_all(cp).wait_recv()
        mine[cp] = jnp.sum(slots[cp], axis=0)
        pair_copy(cp).start()

    sub = iota((per * 8, TILE), 0) % 8
    keeps = [(lane_group == g).astype(F32).astype(BF16) for g in range(per)]

    def turn(at, cols):
        grad = og[at, cols].astype(F32)
        turned = (grad * g_all[at, cols].astype(F32)).astype(BF16)
        cg_all[at, cols] = turned
        return grad, turned

    def outer(ct, b, own, lhs):
        for g in range(per):
            lhs[g * TILE:(g + 1) * TILE] = own * keeps[g]
        window = v_all[b * TILE:(b + 2) * TILE, columns(ct)]
        return dot(lhs[...], window, ((1,), (1,)))

    def fold(products):
        folded = []
        for g in range(per):
            acc = jnp.zeros((8, TILE), F32)
            for a in range(TILE // 8):
                at = slice(a * 8, a * 8 + 8)
                row = slice(g * TILE + a * 8, g * TILE + a * 8 + 8)
                both = jnp.zeros((8, TILE), F32)
                for b, product in products:
                    both = both + product[row, :TILE] * mask_q[b, at, :TILE]
                    both = both + product[row, TILE:] * mask_q[b, at, TILE:]
                acc = acc + pltpu.roll(both, (TILE - 8 * a) % TILE, 1)
            folded.append(acc)
        return jnp.concatenate(folded, axis=0)

    def unskew(table):
        for bit in (1, 2, 4):
            table = jnp.where(sub & bit != 0, pltpu.roll(table, TILE - bit, 1), table)
        return jnp.sum(table.reshape(per, 8, TILE), axis=1)

    def share(cp, sums):
        slots[cp, z] = jnp.concatenate(sums, axis=0)
        for k in sorted(range(1, n_z), key=lambda k: -min(k, n_z - k)):
            z_copy(cp, k).start()

    def main_step(cp, carry):
        @pl.when(cp == 0)
        def _():
            og_copy(6).start()
            hear(2)

        @pl.when(cp == 1)
        def _():
            og_copy(7).start()

        og_copy(2 * cp).wait_recv()
        og_copy(2 * cp + 1).wait_recv()

        grad, turned = turn(slice(0, rows), wide(cp))
        ch_copy(cp).start()
        gate_grad[0, :, wide(cp)] = (grad * conv[:, wide(cp)]).astype(BF16)
        sums = []
        for j in range(2):
            products = []
            for b in range(blocks):
                own = turned[b * TILE:(b + 1) * TILE, j * TILE:(j + 1) * TILE]
                products.append((b, outer(2 * cp + j, b, own, lhs_p.at[j, b])))
            sums.append(unskew(fold(products)))
        share(cp, sums)
        return carry

    lax.fori_loop(0, tiles // 2, main_step, 0)

    def tail_step(cp, carry):
        value_step(cp)
        column_sum(cp)
        return carry

    lax.fori_loop(0, tiles // 2 - 1, tail_step, 0)
    value_step(tiles // 2 - 1)
    column_sum(tiles // 2 - 1)
    for cp in range(tiles // 2):
        pair_copy(cp).wait_recv()
    filter_grad[0] = (mine[...] + theirs[...]).reshape(groups, TILE)

    def sent(ref, sem):
        pltpu.make_async_remote_copy(
            src_ref=ref, dst_ref=ref, send_sem=sem, recv_sem=vh_recv.at[0],
            device_id={"ctx": nxt}, device_id_type=MESH,
        ).wait_send()

    sent(v_all.at[pl.ds(0, TILE)], vh_send)
    sent(og, og_send)
    sent(cg_all.at[pl.ds(0, TILE)], ch_send)
    sent(slots.at[:, pl.ds(0, n_z - 1)], z_send)
    sent(mine, pair_send)


def hand_over(a, b, c, a_out, b_out, c_out, flipped, sems):
    parts = 4
    copies = []
    rows = a.shape[1] // parts
    for i in range(parts):
        at = pl.ds(i * rows, rows)
        copies.append(pltpu.make_async_copy(a.at[0, at], a_out.at[0, at], sems.at[i]))
        copies.append(pltpu.make_async_copy(b.at[0, at], b_out.at[0, at], sems.at[parts + i]))
    for copy in copies:
        copy.start()
    flip = jnp.where(lax.rem(iota((TILE, TILE), 0) + iota((TILE, TILE), 1), TILE) == 0, 1.0, 0.0)
    flipped[0] = lax.dot_general(
        c[0], flip, (((1,), (0,)), ((), ())), precision=lax.Precision.HIGHEST, preferred_element_type=F32
    )
    copies.append(pltpu.make_async_copy(flipped, c_out, sems.at[2 * parts]))
    copies[-1].start()
    for copy in copies:
        copy.wait()


def solution(mesh):
    n_pipe, n_ctx = mesh.shape["pipe"], mesh.shape["ctx"]

    def body(values, gates, incoming, filters, lengths):
        _, rows, width = values.shape
        _, groups, taps = filters.shape
        tiles, blocks = width // TILE, rows // TILE
        chans = width // groups
        per = TILE // chans
        n_z = n_ctx // 2
        dma = pltpu.SemaphoreType.DMA
        any_spec = pl.BlockSpec(memory_space=pl.ANY)
        value_grad, gate_grad, filter_grad = pl.pallas_call(
            functools.partial(kernel, n_pipe, n_ctx, chans),
            out_shape=(
                pltpu.VMEM(values.shape, BF16),
                pltpu.VMEM(values.shape, BF16),
                pltpu.VMEM(filters.shape, F32),
            ),
            in_specs=[pl.BlockSpec(memory_space=pltpu.HBM)] * 5,
            out_specs=(pl.BlockSpec(memory_space=pltpu.VMEM),) * 3,
            scratch_shapes=[
                pltpu.VMEM((rows + TILE, width), BF16),
                pltpu.VMEM((rows, width), BF16),
                pltpu.VMEM((rows, width), BF16),
                pltpu.VMEM((rows + TILE, width), BF16),
                pltpu.VMEM((rows, width), F32),
                pltpu.VMEM((groups, taps), BF16),
                pltpu.SMEM(lengths.shape, jnp.int32),
                pltpu.VMEM((blocks, TILE, 2 * TILE), BF16),
                pltpu.VMEM((blocks, TILE, 2 * TILE), BF16),
                pltpu.VMEM((blocks, TILE, 2 * TILE), F32),
                pltpu.VMEM((tiles, per, taps), F32),
                pltpu.VMEM((tiles, per, taps), F32),
                pltpu.VMEM((per * TILE, 2 * TILE), BF16),
                pltpu.VMEM((per * TILE, 2 * TILE), BF16),
                pltpu.VMEM((tiles, per * TILE, 2 * TILE), BF16),
                pltpu.VMEM((tiles, blocks, per * TILE, 2 * TILE), BF16),
                pltpu.VMEM((2, blocks, per * TILE, TILE), BF16),
                pltpu.VMEM((tiles // 2, n_z, 2 * per, taps), F32),
                pltpu.VMEM((tiles // 2, 2 * per, taps), F32),
                pltpu.VMEM((tiles // 2, 2 * per, taps), F32),
                dma((4,)),
                dma, dma((tiles,)),
                dma, dma((tiles // 2,)),
                dma, dma((tiles // 2,)),
                dma, dma((tiles // 2,)),
                dma, dma((tiles // 2,)),
                pltpu.SemaphoreType.REGULAR((3,)),
            ],
            compiler_params=pltpu.CompilerParams(
                collective_id=0, has_side_effects=True, vmem_limit_bytes=62 * 1024 * 1024
            ),
            cost_estimate=pl.CostEstimate(
                flops=2 * 3 * groups * blocks * TILE * 2 * TILE * TILE,
                bytes_accessed=5 * rows * width * 2, transcendentals=0,
            ),
        )(values, gates, incoming, filters, lengths)
        results = (value_grad, gate_grad, filter_grad)
        return pl.pallas_call(
            hand_over,
            out_shape=tuple(jax.ShapeDtypeStruct(r.shape, r.dtype) for r in results),
            in_specs=[any_spec, any_spec, pl.BlockSpec(memory_space=pltpu.VMEM)],
            out_specs=(any_spec,) * 3,
            scratch_shapes=[pltpu.VMEM(filters.shape, F32), dma((9,))],
            compiler_params=pltpu.CompilerParams(vmem_limit_bytes=4 * 1024 * 1024),
        )(*results)

    shards = P("pipe", "ctx", "tp")
    taps = P("pipe", "tp", None)
    return jax.shard_map(
        body, mesh=mesh, in_specs=(shards, shards, shards, taps, P()), out_specs=(shards, shards, taps), check_vma=False
    )
```
